32 devices in a mesh: grp: 2 (over x), ka: 8 (over z, y), pb: 2 (over core).
Axes of the slice: x: 2, y: 2, z: 4, core: 2. Of those that a mesh axis runs over, the one named last changes fastest.
Arguments:
- momentum_mesh_positions: int32 [3, 8192], P(None, 'ka'), may hold values from 0 to 99
- bravais_translation_list: int32 [512, 3], replicated, may hold values from -4 to 4
- localized_matrix_element_table: bfloat16 [32, 512, 768], P(('grp', 'pb'), 'ka'), parts along dimension 0, may hold values from -0.25 to 0.25
- unitary_band_mixer: bfloat16 [64, 16384], P(None, ('grp', 'ka')), parts along dimension 1, may hold values from -2 to 2
- quasiparticle_level_offsets: bfloat16 [8, 16384], P(None, ('grp', 'ka')), parts along dimension 1, may hold values from -0.3 to 0.3
- displaced_momentum_slot: int32 [32, 8192], P(('grp', 'pb'), 'ka'), parts along dimension 0, may hold values from 0 to 8191, as said below
- vibration_mode_pulsations: bfloat16 [32, 12], P(('grp', 'pb')), parts along dimension 0, may hold values from 0.019897461 to 0.079589844
- occupied_band_tally: int32 [16], P(('grp', 'ka')), parts along dimension 0, may hold values from 1 to 8
- heat_bath_scale: float32 [2], P('grp'), parts along dimension 0, may hold values from 0.02 to 0.06
Outputs:
- self_energy: float32 [8, 16384], P(None, ('grp', 'ka')), parts along dimension 1
- linewidth: float32 [32, 12], P(('grp', 'pb')), parts along dimension 0
The draws below stay inside these ranges and needn't reach their ends.
There are 2 independent parts, one for each index of `grp`. The reference program is written for one: setup_inputs(seed, part) draws one part's arguments, and reference() takes and returns one part's arrays. A program takes and returns all parts, laid end to end along the dimension named above; an argument that names none is the same for every part. Nothing has to cross between parts.
Inputs may be any that keep to these rules, and one draw needn't show every extreme that they name: For each q, displaced_momentum_slot[q, k] = (k + s_q) mod 8192 with one shift s_q for that q.
All inputs are finite; a program needn't handle non-finite values.
Results may differ from the reference program's by a relative error of at most 0.0022.
Values may be sent and summed in bfloat16 or wider, within the bound.
A program may use at most 128 MiB of HBM per device.

```python
import math
import jax
import jax.numpy as jnp
from jax import lax

NB = 8
NM = 12
NR = 512
KDEV = 1024
KTOT = 8192
QTOT = 16
FEAT = 768
KBLOCKS = 8


def draw_momentum_mesh_positions(key, part):
    key = jax.random.fold_in(key, 11)
    return jax.random.randint(key, (3, KTOT), 0, 100, dtype=jnp.int32)


def draw_displaced_momentum_slot(key, part):
    key = jax.random.fold_in(key, 23)
    key_blocks, key_order, key_rest = jax.random.split(key, 3)
    blocks = jax.random.randint(key_blocks, (QTOT,), 0, KBLOCKS, dtype=jnp.int32)
    order = jax.random.permutation(key_order, QTOT).astype(jnp.int32)
    blocks = jnp.where(order == 0, KBLOCKS // 2, jnp.where(order == 1, KBLOCKS - 1, blocks)).astype(jnp.int32)
    rest = jax.random.randint(key_rest, (QTOT,), 0, KDEV, dtype=jnp.int32)
    shifts = (blocks * KDEV + rest).astype(jnp.int32)
    rows = jnp.arange(KTOT, dtype=jnp.int32)
    return ((rows[None, :] + shifts[:, None]) % KTOT).astype(jnp.int32)


def draw_quasiparticle_level_offsets(key, part):
    key = jax.random.fold_in(key, 31)
    key_sign, key_size = jax.random.split(key, 2)
    size = jax.random.uniform(key_size, (NB, KTOT), jnp.float32, 0.25, 0.2988)
    sign = jnp.where(jax.random.bernoulli(key_sign, 0.5, (NB, KTOT)), 1.0, -1.0).astype(jnp.float32)
    levels = sign * size
    return levels.astype(jnp.bfloat16)


def draw_heat_bath_scale(key, part):
    key = jax.random.fold_in(key, 37)
    scale = jax.random.uniform(key, (1,), jnp.float32, 0.02, 0.06)
    return scale.astype(jnp.float32)


def with_ends(array, rng, smallest, top_value):
    longest = array.shape.index(max(array.shape))
    spots = []
    for shift in (0, 1):
        where = [jax.random.randint(jax.random.fold_in(rng, axis), (), 0, length) for axis, length in enumerate(array.shape)]
        where[longest] = (where[longest] + shift) % array.shape[longest]
        spots.append(tuple(where))
    return array.at[spots[0]].set(smallest).at[spots[1]].set(top_value)


def steps_of(rng, shape, pieces, least, top_value):
    def one(position, parts):
        heights = jax.random.uniform(jax.random.fold_in(jax.random.fold_in(rng, 6), position), (parts,), jnp.float32, least / len(pieces), top_value / len(pieces))
        return jnp.repeat(jnp.exp(heights), shape[position] // parts).reshape((-1,) + (1,) * (len(shape) - position - 1))

    factor_of = one(*pieces[0])
    for cut in pieces[1:]:
        factor_of = factor_of * one(*cut)
    return factor_of


def noise(rng, extent, spread, bound, pieces=(), held_as=jnp.bfloat16):
    drawn = jax.random.normal(rng, extent, jnp.float32) * spread
    if len(pieces) > 0:
        drawn = steps_of(rng, extent, pieces, -0.22, 0.18) * drawn
    return jnp.clip(drawn, min=-bound, max=bound).astype(held_as)


def setup_inputs(seed: int = 0, part: int = 0) -> dict:
    seeds = jax.random.split(jax.random.key(seed), 10)
    own_keys = jax.random.split(jax.random.fold_in(seeds[9], part), 10)
    return {
        "momentum_mesh_positions": draw_momentum_mesh_positions(jax.random.fold_in(seeds[9], 71), part),
        "bravais_translation_list": with_ends(jax.random.randint(seeds[1], (NR, 3), -4, 5), jax.random.fold_in(seeds[1], 1), -4, 4).astype(jnp.int32),
        "localized_matrix_element_table": noise(own_keys[2], (QTOT, NR, FEAT), NR ** -0.5, 0.25, ((0, 2), (1, 8))),
        "unitary_band_mixer": noise(own_keys[3], (NB * NB, KTOT), NB ** -0.5, 2.0, ((1, 8),)),
        "quasiparticle_level_offsets": draw_quasiparticle_level_offsets(jax.random.fold_in(jax.random.fold_in(seeds[9], part), 71), part),
        "displaced_momentum_slot": draw_displaced_momentum_slot(jax.random.fold_in(jax.random.fold_in(seeds[9], part), 71), part),
        "vibration_mode_pulsations": jnp.clip(jnp.exp(math.log(0.079589844) - 1.3862944 * jax.random.uniform(own_keys[6], (QTOT, NM), jnp.float32) ** steps_of(own_keys[6], (QTOT, NM), ((0, 2),), -0.2, 0.2)), 0.019897461, 0.079589844).astype(jnp.bfloat16),
        "occupied_band_tally": with_ends(jax.random.randint(own_keys[7], (KBLOCKS,), 1, NB + 1), jax.random.fold_in(own_keys[7], 1), 1, NB).astype(jnp.int32),
        "heat_bath_scale": draw_heat_bath_scale(jax.random.fold_in(jax.random.fold_in(seeds[9], part), 71), part),
    }


ETA = 0.05


def phases(momentum_mesh_positions, bravais_translation_list):
    product = (momentum_mesh_positions[0][:, None] * bravais_translation_list[:, 0][None, :]
               + momentum_mesh_positions[1][:, None] * bravais_translation_list[:, 1][None, :]
               + momentum_mesh_positions[2][:, None] * bravais_translation_list[:, 2][None, :])
    product = product % 100
    return jnp.cos(product.astype(jnp.float32) * (2.0 * math.pi / 100.0)).astype(jnp.bfloat16)


def lorentz(value):
    return (ETA / math.pi) / (value * value + ETA * ETA)


def couple(interp, kq_rows, mode_freq, e_here, u_here, fermi_here, band_mask, eig_all, en_all, occupation_multiplier):
    row_count = interp.shape[0]
    coupling = interp.reshape(row_count, NM, NB, NB).astype(jnp.float32)
    u_far = jnp.take(eig_all, kq_rows, axis=1).astype(jnp.float32).T.reshape(row_count, NB, NB)
    e_far = jnp.take(en_all, kq_rows, axis=1).astype(jnp.float32).T
    inner = jnp.einsum('kvab,kbn->kvan', coupling, u_here, precision=lax.Precision.HIGHEST).astype(jnp.bfloat16)
    rotated = jnp.einsum('kam,kvan->kvmn', u_far, inner.astype(jnp.float32), precision=lax.Precision.HIGHEST)
    squared = rotated * rotated
    fermi_far = 1.0 / (1.0 + jnp.exp(e_far / occupation_multiplier))
    bose = 1.0 / (jnp.exp(mode_freq / occupation_multiplier) - 1.0)
    energy_gap = e_here[:, None, None, :] - e_far[:, None, :, None]
    mode_term = mode_freq[None, :, None, None]
    plus = lorentz(energy_gap + mode_term)
    minus = lorentz(energy_gap - mode_term)
    bose_term = bose[None, :, None, None]
    fermi_m = fermi_far[:, None, :, None]
    kpoint_weight = (bose_term + fermi_m) * plus + (bose_term + 1.0 - fermi_m) * minus
    self_term = jnp.sum(squared * kpoint_weight, axis=(1, 2))
    flow = band_mask[:, None, None, :] * (fermi_here[:, None, None, :] - fermi_m) * plus
    width_term = 2.0 * math.pi * mode_freq * jnp.sum(squared * flow, axis=(0, 2, 3))
    return self_term, width_term


def reference(momentum_mesh_positions, bravais_translation_list, localized_matrix_element_table, unitary_band_mixer, quasiparticle_level_offsets, displaced_momentum_slot, vibration_mode_pulsations, occupied_band_tally, heat_bath_scale):
    occupation_multiplier = heat_bath_scale[0]
    phase = phases(momentum_mesh_positions, bravais_translation_list)
    u_here = unitary_band_mixer.astype(jnp.float32).T.reshape(KTOT, NB, NB)
    e_here = quasiparticle_level_offsets.astype(jnp.float32).T
    fermi_here = 1.0 / (1.0 + jnp.exp(e_here / occupation_multiplier))
    block_of = (jnp.arange(KTOT, dtype=jnp.int32) // KDEV).astype(jnp.int32)
    window_top = jnp.take(occupied_band_tally, block_of)
    band_mask = (jnp.arange(NB, dtype=jnp.int32)[None, :] < window_top[:, None]).astype(jnp.float32)

    def advance(running, inputs):
        coupling_one, kq_rows, mode_freq = inputs
        interp = jnp.dot(phase, coupling_one, preferred_element_type=jnp.float32).astype(jnp.bfloat16)
        self_term, width_term = couple(interp, kq_rows, mode_freq.astype(jnp.float32), e_here, u_here,
                                       fermi_here, band_mask, unitary_band_mixer, quasiparticle_level_offsets, occupation_multiplier)
        return running + self_term, width_term

    running, widths = lax.scan(advance, jnp.zeros((KTOT, NB), jnp.float32), (localized_matrix_element_table, displaced_momentum_slot, vibration_mode_pulsations))
    self_energy = (band_mask * running / (QTOT * NM)).T
    linewidth = widths / KTOT
    return self_energy, linewidth
```

```python
import functools
import math

import jax
import jax.numpy as jnp
from jax import lax
from jax.experimental import pallas as pl
from jax.experimental.pallas import tpu as pltpu
from jax.sharding import PartitionSpec as P

NB = 8
NM = 12
ETA = 0.05
ROWS = 80
MESH = pl.DeviceIdType.MESH
SIN = (6.28318516, -41.3416549, 81.6009982, -76.5496568, 39.5358137)


def exchange(pack_ref, table_ref, all_ref, part_ref, send_pack, recv_pack, send_part, recv_part, own_sems):
    count = all_ref.shape[0]
    per_q = count // table_ref.shape[0]
    me = lax.axis_index("ka")
    barrier = pltpu.get_barrier_semaphore()

    def greet(step, carry):
        pl.semaphore_signal(barrier, inc=1, device_id={"ka": lax.rem(me + step, count)}, device_id_type=MESH)
        return carry

    lax.fori_loop(1, count, greet, 0)
    pl.semaphore_wait(barrier, count - 1)

    def copies(step, sender):
        peer = lax.rem(me + step, count)
        block = pltpu.make_async_remote_copy(
            src_ref=pack_ref,
            dst_ref=all_ref.at[sender],
            send_sem=send_pack.at[step],
            recv_sem=recv_pack.at[sender],
            device_id={"ka": peer},
            device_id_type=MESH,
        )
        cells = pltpu.make_async_remote_copy(
            src_ref=table_ref.at[peer // per_q],
            dst_ref=part_ref.at[sender],
            send_sem=send_part.at[step],
            recv_sem=recv_part.at[sender],
            device_id={"ka": peer},
            device_id_type=MESH,
        )
        return block, cells

    def start(step, carry):
        block, cells = copies(step, me)
        block.start()
        cells.start()
        return carry

    lax.fori_loop(1, count, start, 0)
    own = (
        pltpu.make_async_copy(pack_ref, all_ref.at[me], own_sems.at[0]),
        pltpu.make_async_copy(table_ref.at[me // per_q], part_ref.at[me], own_sems.at[1]),
    )
    for copy in own:
        copy.start()
    for copy in own:
        copy.wait()

    def finish(step, carry):
        block, cells = copies(step, me)
        block.wait_send()
        cells.wait_send()
        block, cells = copies(step, lax.rem(me + step, count))
        block.wait_recv()
        cells.wait_recv()
        return carry

    lax.fori_loop(1, count, finish, 0)


def couple(
    where_ref,
    mode_ref,
    all_ref,
    part_ref,
    cell_ref,
    sigma_ref,
    width_ref,
    interp,
    near,
    far,
    level,
    acc,
):
    block = where_ref[1] + pl.program_id(0)
    chunks = all_ref.shape[0] * 8
    inv_t = mode_ref[3, 0]

    @pl.when(pl.program_id(0) == 0)
    def _():
        acc[...] = jnp.zeros_like(acc)

    product = jnp.dot(cell_ref[...], all_ref[block, 64:80, :], preferred_element_type=jnp.float32)
    turn = product * 0.01
    turn = jnp.abs(turn - jnp.floor(turn + 0.5))
    angle = 0.25 - turn
    square = angle * angle
    value = SIN[4]
    for coefficient in (SIN[3], SIN[2], SIN[1], SIN[0]):
        value = value * square + coefficient
    phase = (value * angle).astype(jnp.bfloat16)
    folded = lax.dot_general(part_ref[...], phase, (((0,), (0,)), ((), ())), preferred_element_type=jnp.float32)
    for c in range(8):
        interp[pl.ds(c, 64 * NM, stride=8), :] = folded[:, c * 128 : (c + 1) * 128]

    for c in range(8):
        near[pl.ds(c, ROWS, stride=8), :] = all_ref[block, :, c * 128 : (c + 1) * 128].astype(jnp.float32)
    offset = lax.rem(block * 1024 + where_ref[0], chunks * 128)
    first, inside = offset // 128, lax.rem(offset, 128)
    lanes = lax.broadcasted_iota(jnp.int32, (ROWS, 128), 1)

    def turned(c):
        index = lax.rem(first + c, chunks)
        lane = pl.multiple_of(lax.rem(index, 8) * 128, 128)
        raw = all_ref[index // 8, :, pl.ds(lane, 128)].astype(jnp.float32)
        return pltpu.roll(raw, lax.rem(128 - inside, 128), 1)

    here = turned(0)
    for c in range(8):
        after = turned(c + 1)
        far[pl.ds(c, ROWS, stride=8), :] = jnp.where(lanes < 128 - inside, here, after)
        here = after

    def row(ref, index):
        return ref[pl.ds(pl.multiple_of(index * 8, 8), 8), :]

    def fermi(energy):
        return 1.0 / (1.0 + jnp.exp(energy * inv_t))

    for m in range(NB):
        level[pl.ds(m * 8, 8), :] = fermi(row(far, 64 + m))
    tally = row(near, 75)

    def over_n(n, carry):
        e_n = row(near, 64 + n)
        f_n = fermi(e_n)
        mask = jnp.where(n.astype(jnp.float32) < tally, 1.0, 0.0)
        for m in range(NB):
            gap = e_n - row(far, 64 + m)
            level[pl.ds(64 + m * 8, 8), :] = gap * gap + ETA * ETA
            level[pl.ds(128 + m * 8, 8), :] = gap + gap
            level[pl.ds(192 + m * 8, 8), :] = mask * (f_n - row(level, m))
            level[pl.ds(256 + m * 8, 8), :] = (1.0 - 2.0 * row(level, m)) * (gap + gap)
        u_n = [row(near, b * NB + n) for b in range(NB)]

        def over_v(v, total):
            w = mode_ref[0, v]
            w2 = mode_ref[1, v]
            twice = mode_ref[2, v]
            inner = []
            for a in range(NB):
                term = row(interp, v * 64 + a * 8) * u_n[0]
                for b in range(1, NB):
                    term = term + row(interp, v * 64 + a * 8 + b) * u_n[b]
                inner.append(term)
            width = jnp.zeros((8, 128), jnp.float32)
            for m in range(NB):
                rotated = row(far, m) * inner[0]
                for a in range(1, NB):
                    rotated = rotated + row(far, a * NB + m) * inner[a]
                even = row(level, 8 + m) + w2
                odd = row(level, 16 + m) * w
                low = even - odd
                high = even + odd
                scaled = rotated * rotated * pl.reciprocal(low * high)
                total = total + scaled * (twice * even + w * row(level, 32 + m))
                width = width + row(level, 24 + m) * (low * scaled)
            spot = pl.ds(pl.multiple_of(v * 8, 8), 8)
            acc[spot, :] = acc[spot, :] + width
            return total

        total = lax.fori_loop(0, NM, over_v, jnp.zeros((8, 128), jnp.float32))
        sigma_ref[0, pl.ds(pl.multiple_of(n * 8, 8), 8), :] = mask * total
        return carry

    lax.fori_loop(0, NB, over_n, 0)

    @pl.when(pl.program_id(0) == pl.num_programs(0) - 1)
    def _():
        lane = lax.broadcasted_iota(jnp.int32, (8, 128), 1)
        out = jnp.zeros((8, 128), jnp.float32)
        for v in range(NM):
            out = out + jnp.where(lane == v, jnp.sum(acc[v * 8 : v * 8 + 8, :]), 0.0)
        width_ref[...] = out


def collect(q_local, sigma_ref, width_ref, total_ref, widths_ref, got, got_w, send_s, recv_s, send_w, recv_w, own_sems):
    count = got_w.shape[0]
    cores = got.shape[0] // q_local
    per_q = count // q_local
    me, core = lax.axis_index("ka"), lax.axis_index("pb")
    everyone = count * cores
    mine = me * cores + core
    barrier = pltpu.get_barrier_semaphore()

    def greet(step, carry):
        other = lax.rem(mine + step, everyone)
        pl.semaphore_signal(
            barrier, inc=1, device_id={"ka": other // cores, "pb": lax.rem(other, cores)}, device_id_type=MESH
        )
        return carry

    lax.fori_loop(1, everyone, greet, 0)
    pl.semaphore_wait(barrier, everyone - 1)

    q_mine, range_mine = me // per_q, lax.rem(me, per_q)
    slot_mine = core * q_local + q_mine

    def sigma_copy(index, slot):
        b, to_core = index // cores, lax.rem(index, cores)
        return pltpu.make_async_remote_copy(
            src_ref=sigma_ref.at[b],
            dst_ref=got.at[slot],
            send_sem=send_s.at[index],
            recv_sem=recv_s.at[slot],
            device_id={"ka": range_mine * q_local + b, "pb": to_core},
            device_id_type=MESH,
        )

    def width_copy(step, sender):
        return pltpu.make_async_remote_copy(
            src_ref=width_ref,
            dst_ref=got_w.at[sender],
            send_sem=send_w.at[step],
            recv_sem=recv_w.at[sender],
            device_id={"ka": lax.rem(me + step, count)},
            device_id_type=MESH,
        )

    def start_s(index, carry):
        target = (range_mine * q_local + index // cores) * cores + lax.rem(index, cores)

        @pl.when(target != mine)
        def _():
            sigma_copy(index, slot_mine).start()

        @pl.when(target == mine)
        def _():
            copy = pltpu.make_async_copy(sigma_ref.at[index // cores], got.at[slot_mine], own_sems.at[0])
            copy.start()
            copy.wait()

        return carry

    lax.fori_loop(0, q_local * cores, start_s, 0)

    def start_w(step, carry):
        width_copy(step, me).start()
        return carry

    lax.fori_loop(1, count, start_w, 0)
    copy = pltpu.make_async_copy(width_ref, got_w.at[me], own_sems.at[1])
    copy.start()
    copy.wait()

    def finish_s(index, carry):
        target = (range_mine * q_local + index // cores) * cores + lax.rem(index, cores)

        @pl.when(target != mine)
        def _():
            sigma_copy(index, slot_mine).wait_send()

        from_core, from_q = index // q_local, lax.rem(index, q_local)
        source = (from_q * per_q + me // q_local) * cores + from_core

        @pl.when(source != mine)
        def _():
            sigma_copy(index, index).wait_recv()

        return carry

    lax.fori_loop(0, q_local * cores, finish_s, 0)

    def finish_w(step, carry):
        width_copy(step, me).wait_send()
        width_copy(step, lax.rem(me + step, count)).wait_recv()
        return carry

    lax.fori_loop(1, count, finish_w, 0)
    total = got[0]
    for slot in range(1, q_local * cores):
        total = total + got[slot]
    total_ref[...] = total
    for q in range(q_local):
        width = got_w[q * per_q]
        for part in range(1, per_q):
            width = width + got_w[q * per_q + part]
        widths_ref[q, :, :] = width


def on_device(
    momentum_mesh_positions,
    bravais_translation_list,
    localized_matrix_element_table,
    unitary_band_mixer,
    quasiparticle_level_offsets,
    displaced_momentum_slot,
    vibration_mode_pulsations,
    occupied_band_tally,
    heat_bath_scale,
):
    kcount = momentum_mesh_positions.shape[1]
    q_local, cells, feat = localized_matrix_element_table.shape
    count, cores = lax.axis_size("ka"), lax.axis_size("pb")
    k_total = kcount * count
    per_q = count // q_local
    me = lax.axis_index("ka")
    tau = heat_bath_scale[0]
    pack = jnp.concatenate(
        [
            unitary_band_mixer,
            quasiparticle_level_offsets,
            momentum_mesh_positions.astype(jnp.bfloat16),
            jnp.broadcast_to(occupied_band_tally.astype(jnp.bfloat16)[:, None], (1, kcount)),
            jnp.zeros((4, kcount), jnp.bfloat16),
        ],
        axis=0,
    )
    q_mine = me // per_q
    slot = lax.dynamic_slice(displaced_momentum_slot, (q_mine, 0), (1, 1))[0, 0]
    shift = jnp.mod(slot - me * kcount, k_total)
    where = jnp.stack([shift, lax.rem(me, per_q) * q_local]).astype(jnp.int32)
    freq_own = vibration_mode_pulsations.astype(jnp.float32)
    freq = lax.dynamic_slice_in_dim(freq_own, q_mine, 1, 0)[0]
    twice = 2.0 / (jnp.exp(freq / tau) - 1.0) + 1.0
    modes = jnp.stack([freq, freq * freq, twice, jnp.broadcast_to(1.0 / tau, (NM,))])
    cell_rows = jnp.pad(bravais_translation_list.astype(jnp.bfloat16), ((0, 0), (8, 5)))

    anywhere = pl.BlockSpec(memory_space=pl.ANY)
    in_vmem = pl.BlockSpec(memory_space=pltpu.VMEM)
    in_smem = pl.BlockSpec(memory_space=pltpu.SMEM)
    packs, part = pl.pallas_call(
        exchange,
        out_shape=(
            jax.ShapeDtypeStruct((count, ROWS, kcount), jnp.bfloat16),
            jax.ShapeDtypeStruct((count, cells, feat), jnp.bfloat16),
        ),
        in_specs=[anywhere] * 2,
        out_specs=(anywhere, anywhere),
        scratch_shapes=[pltpu.SemaphoreType.DMA((count,))] * 4 + [pltpu.SemaphoreType.DMA((2,))],
        compiler_params=pltpu.CompilerParams(collective_id=0, has_side_effects=True),
    )(pack, localized_matrix_element_table)

    sigma, width = pl.pallas_call(
        couple,
        grid=(q_local,),
        out_shape=(
            jax.ShapeDtypeStruct((q_local, NB * 8, 128), jnp.float32),
            jax.ShapeDtypeStruct((8, 128), jnp.float32),
        ),
        in_specs=[in_smem, in_smem, in_vmem, in_vmem, in_vmem],
        out_specs=(
            pl.BlockSpec((1, NB * 8, 128), lambda i: (i, 0, 0)),
            pl.BlockSpec((8, 128), lambda i: (0, 0)),
        ),
        scratch_shapes=[
            pltpu.VMEM((64 * NM * 8, 128), jnp.float32),
            pltpu.VMEM((ROWS * 8, 128), jnp.float32),
            pltpu.VMEM((ROWS * 8, 128), jnp.float32),
            pltpu.VMEM((5 * 64, 128), jnp.float32),
            pltpu.VMEM((NM * 8, 128), jnp.float32),
        ],
        compiler_params=pltpu.CompilerParams(vmem_limit_bytes=48 * 1024 * 1024),
    )(where, modes, packs, part.reshape(count * cells, feat), cell_rows)

    total, widths = pl.pallas_call(
        functools.partial(collect, q_local),
        out_shape=(
            jax.ShapeDtypeStruct((NB * 8, 128), jnp.float32),
            jax.ShapeDtypeStruct((q_local, 8, 128), jnp.float32),
        ),
        in_specs=[in_vmem] * 2,
        out_specs=(in_vmem, in_vmem),
        scratch_shapes=[
            pltpu.VMEM((cores * q_local, NB * 8, 128), jnp.float32),
            pltpu.VMEM((count, 8, 128), jnp.float32),
            pltpu.SemaphoreType.DMA((cores * q_local,)),
            pltpu.SemaphoreType.DMA((cores * q_local,)),
            pltpu.SemaphoreType.DMA((count,)),
            pltpu.SemaphoreType.DMA((count,)),
            pltpu.SemaphoreType.DMA((2,)),
        ],
        compiler_params=pltpu.CompilerParams(collective_id=1, has_side_effects=True),
    )(sigma, width)
    scale = ETA / math.pi
    self_energy = total.reshape(NB, kcount) * (scale / (q_local * cores * NM))
    linewidth = widths[:, 0, :NM] * freq_own * (2.0 * math.pi * scale / k_total)
    return (self_energy, linewidth)


def solution(mesh):
    return jax.shard_map(
        on_device,
        mesh=mesh,
        in_specs=(
            P(None, "ka"),
            P(),
            P(("grp", "pb"), "ka", None),
            P(None, ("grp", "ka")),
            P(None, ("grp", "ka")),
            P(("grp", "pb"), "ka"),
            P(("grp", "pb"), None),
            P(("grp", "ka")),
            P("grp"),
        ),
        out_specs=(P(None, ("grp", "ka")), P(("grp", "pb"), None)),
        check_vma=False,
    )
```

```python
import functools
import math

import jax
import jax.numpy as jnp
from jax import lax
from jax.experimental import pallas as pl
from jax.experimental.pallas import tpu as pltpu
from jax.sharding import PartitionSpec as P

NB = 8
NM = 12
ETA = 0.05
ROWS = 80
MESH = pl.DeviceIdType.MESH
SIN = (6.28318516, -41.3416549, 81.6009982, -76.5496568, 39.5358137)


def exchange(pack_ref, table_ref, all_ref, part_ref, send_pack, recv_pack, send_part, recv_part, own_sems):
    count = all_ref.shape[0]
    per_q = count // table_ref.shape[0]
    me = lax.axis_index("ka")
    barrier = pltpu.get_barrier_semaphore()

    def greet(step, carry):
        pl.semaphore_signal(barrier, inc=1, device_id={"ka": lax.rem(me + step, count)}, device_id_type=MESH)
        return carry

    lax.fori_loop(1, count, greet, 0)
    pl.semaphore_wait(barrier, count - 1)

    def copies(step, sender):
        peer = lax.rem(me + step, count)
        block = pltpu.make_async_remote_copy(
            src_ref=pack_ref,
            dst_ref=all_ref.at[sender],
            send_sem=send_pack.at[step],
            recv_sem=recv_pack.at[sender],
            device_id={"ka": peer},
            device_id_type=MESH,
        )
        cells = pltpu.make_async_remote_copy(
            src_ref=table_ref.at[peer // per_q],
            dst_ref=part_ref.at[sender],
            send_sem=send_part.at[step],
            recv_sem=recv_part.at[sender],
            device_id={"ka": peer},
            device_id_type=MESH,
        )
        return block, cells

    def start(step, carry):
        block, cells = copies(step, me)
        block.start()
        cells.start()
        return carry

    lax.fori_loop(1, count, start, 0)
    own = (
        pltpu.make_async_copy(pack_ref, all_ref.at[me], own_sems.at[0]),
        pltpu.make_async_copy(table_ref.at[me // per_q], part_ref.at[me], own_sems.at[1]),
    )
    for copy in own:
        copy.start()
    for copy in own:
        copy.wait()

    def finish(step, carry):
        block, cells = copies(step, me)
        block.wait_send()
        cells.wait_send()
        block, cells = copies(step, lax.rem(me + step, count))
        block.wait_recv()
        cells.wait_recv()
        return carry

    lax.fori_loop(1, count, finish, 0)


def couple(
    where_ref,
    mode_ref,
    all_ref,
    part_ref,
    cell_ref,
    sigma_ref,
    width_ref,
    wide,
    interp,
    near,
    far,
    u_near,
    u_far,
    level,
    sums,
    acc,
):
    block = where_ref[1] + pl.program_id(0)
    chunks = all_ref.shape[0] * 8
    inv_t = mode_ref[3, 0]

    @pl.when(pl.program_id(0) == 0)
    def _():
        acc[...] = jnp.zeros_like(acc)

    product = jnp.dot(cell_ref[...], all_ref[block, 64:80, :], preferred_element_type=jnp.float32)
    turn = product * 0.01
    turn = jnp.abs(turn - jnp.floor(turn + 0.5))
    angle = 0.25 - turn
    square = angle * angle
    value = SIN[4]
    for coefficient in (SIN[3], SIN[2], SIN[1], SIN[0]):
        value = value * square + coefficient
    phase = (value * angle).astype(jnp.bfloat16)
    folded = lax.dot_general(part_ref[...], phase, (((0,), (0,)), ((), ())), preferred_element_type=jnp.float32)
    for pair in range(NM // 2):
        for half in range(2):
            mode = 2 * pair + half
            for c in range(8):
                wide[pl.ds(pair * 1024 + half * 8 + c, 64, stride=16), :] = folded[
                    mode * 64 : mode * 64 + 64, c * 128 : (c + 1) * 128
                ]
    interp[...] = wide[...].astype(jnp.bfloat16)

    def spread(narrow_ref, c, rows):
        narrow_ref[pl.ds(c, 16, stride=8), :] = rows[64:ROWS]
        wide[pl.ds(c, 64, stride=16), :] = rows[0:64]
        wide[pl.ds(8 + c, 64, stride=16), :] = rows[0:64]

    for c in range(8):
        spread(near, c, all_ref[block, :, c * 128 : (c + 1) * 128].astype(jnp.float32))
    u_near[...] = wide[0:1024, :].astype(jnp.bfloat16)
    offset = lax.rem(block * 1024 + where_ref[0], chunks * 128)
    first, inside = offset // 128, lax.rem(offset, 128)
    lanes = lax.broadcasted_iota(jnp.int32, (ROWS, 128), 1)

    def turned(c):
        index = lax.rem(first + c, chunks)
        lane = pl.multiple_of(lax.rem(index, 8) * 128, 128)
        raw = all_ref[index // 8, :, pl.ds(lane, 128)].astype(jnp.float32)
        return pltpu.roll(raw, lax.rem(128 - inside, 128), 1)

    here = turned(0)
    for c in range(8):
        after = turned(c + 1)
        spread(far, c, jnp.where(lanes < 128 - inside, here, after))
        here = after
    u_far[...] = wide[0:1024, :].astype(jnp.bfloat16)

    def row(ref, index):
        return ref[pl.ds(pl.multiple_of(index * 8, 8), 8), :]

    def pair_row(ref, index):
        return ref[pl.ds(pl.multiple_of(index * 16, 16), 16), :]

    def fermi(energy):
        return 1.0 / (1.0 + jnp.exp(energy * inv_t))

    for m in range(NB):
        level[pl.ds(m * 8, 8), :] = fermi(row(far, m))
    tally = row(near, 11)

    def over_n(n, carry):
        e_n = row(near, n)
        f_n = fermi(e_n)
        mask = jnp.where(n.astype(jnp.float32) < tally, 1.0, 0.0)
        for m in range(NB):
            gap = e_n - row(far, m)
            level[pl.ds(64 + m * 8, 8), :] = gap * gap + ETA * ETA
            level[pl.ds(128 + m * 8, 8), :] = gap + gap
            level[pl.ds(192 + m * 8, 8), :] = mask * (f_n - row(level, m))
            level[pl.ds(256 + m * 8, 8), :] = (1.0 - 2.0 * row(level, m)) * (gap + gap)
        u_n = [pair_row(u_near, b * NB + n) for b in range(NB)]

        def over_pairs(pair, total):
            inner = []
            for a in range(NB):
                term = pair_row(interp, pair * 64 + a * 8) * u_n[0]
                for b in range(1, NB):
                    term = term + pair_row(interp, pair * 64 + a * 8 + b) * u_n[b]
                inner.append(term)
            widths = [jnp.zeros((8, 128), jnp.float32) for _ in range(2)]
            for m in range(NB):
                rotated = pair_row(u_far, m) * inner[0]
                for a in range(1, NB):
                    rotated = rotated + pair_row(u_far, a * NB + m) * inner[a]
                rotated = rotated.astype(jnp.float32)
                for half in range(2):
                    v = 2 * pair + half
                    w = mode_ref[0, v]
                    own = rotated[half * 8 : half * 8 + 8]
                    even = row(level, 8 + m) + mode_ref[1, v]
                    odd = row(level, 16 + m) * w
                    low = even - odd
                    high = even + odd
                    scaled = own * own * pl.reciprocal(low * high, approx=True)
                    total = total + scaled * (mode_ref[2, v] * even + w * row(level, 32 + m))
                    widths[half] = widths[half] + row(level, 24 + m) * (low * scaled)
            for half in range(2):
                spot = pl.ds(pl.multiple_of(pair * 16, 16) + half * 8, 8)
                acc[spot, :] = acc[spot, :] + widths[half]
            return total

        total = lax.fori_loop(0, NM // 2, over_pairs, jnp.zeros((8, 128), jnp.float32))
        sums[pl.ds(pl.multiple_of(n * 8, 8), 8), :] = mask * total
        return carry

    lax.fori_loop(0, NB, over_n, 0)
    sigma_ref[0] = sums[...].astype(jnp.bfloat16)

    @pl.when(pl.program_id(0) == pl.num_programs(0) - 1)
    def _():
        lane = lax.broadcasted_iota(jnp.int32, (8, 128), 1)
        out = jnp.zeros((8, 128), jnp.float32)
        for v in range(NM):
            out = out + jnp.where(lane == v, jnp.sum(acc[v * 8 : v * 8 + 8, :]), 0.0)
        width_ref[...] = out


def collect(q_local, sigma_ref, width_ref, total_ref, widths_ref, got, got_w, send_s, recv_s, send_w, recv_w, own_sems):
    count = got_w.shape[0]
    cores = got.shape[0] // q_local
    per_q = count // q_local
    me, core = lax.axis_index("ka"), lax.axis_index("pb")
    everyone = count * cores
    mine = me * cores + core
    barrier = pltpu.get_barrier_semaphore()

    def greet(step, carry):
        other = lax.rem(mine + step, everyone)
        pl.semaphore_signal(
            barrier, inc=1, device_id={"ka": other // cores, "pb": lax.rem(other, cores)}, device_id_type=MESH
        )
        return carry

    lax.fori_loop(1, everyone, greet, 0)
    pl.semaphore_wait(barrier, everyone - 1)

    q_mine, range_mine = me // per_q, lax.rem(me, per_q)
    slot_mine = core * q_local + q_mine

    def sigma_copy(index, slot):
        b, to_core = index // cores, lax.rem(index, cores)
        return pltpu.make_async_remote_copy(
            src_ref=sigma_ref.at[b],
            dst_ref=got.at[slot],
            send_sem=send_s.at[index],
            recv_sem=recv_s.at[slot],
            device_id={"ka": range_mine * q_local + b, "pb": to_core},
            device_id_type=MESH,
        )

    def width_copy(step, sender):
        return pltpu.make_async_remote_copy(
            src_ref=width_ref,
            dst_ref=got_w.at[sender],
            send_sem=send_w.at[step],
            recv_sem=recv_w.at[sender],
            device_id={"ka": lax.rem(me + step, count)},
            device_id_type=MESH,
        )

    def start_s(index, carry):
        target = (range_mine * q_local + index // cores) * cores + lax.rem(index, cores)

        @pl.when(target != mine)
        def _():
            sigma_copy(index, slot_mine).start()

        @pl.when(target == mine)
        def _():
            copy = pltpu.make_async_copy(sigma_ref.at[index // cores], got.at[slot_mine], own_sems.at[0])
            copy.start()
            copy.wait()

        return carry

    lax.fori_loop(0, q_local * cores, start_s, 0)

    def start_w(step, carry):
        width_copy(step, me).start()
        return carry

    lax.fori_loop(1, count, start_w, 0)
    copy = pltpu.make_async_copy(width_ref, got_w.at[me], own_sems.at[1])
    copy.start()
    copy.wait()

    def finish_s(index, carry):
        target = (range_mine * q_local + index // cores) * cores + lax.rem(index, cores)

        @pl.when(target != mine)
        def _():
            sigma_copy(index, slot_mine).wait_send()

        from_core, from_q = index // q_local, lax.rem(index, q_local)
        source = (from_q * per_q + me // q_local) * cores + from_core

        @pl.when(source != mine)
        def _():
            sigma_copy(index, index).wait_recv()

        return carry

    lax.fori_loop(0, q_local * cores, finish_s, 0)

    def finish_w(step, carry):
        width_copy(step, me).wait_send()
        width_copy(step, lax.rem(me + step, count)).wait_recv()
        return carry

    lax.fori_loop(1, count, finish_w, 0)
    total = got[0].astype(jnp.float32)
    for slot in range(1, q_local * cores):
        total = total + got[slot].astype(jnp.float32)
    total_ref[...] = total
    for q in range(q_local):
        width = got_w[q * per_q]
        for part in range(1, per_q):
            width = width + got_w[q * per_q + part]
        widths_ref[q, :, :] = width


def on_device(
    momentum_mesh_positions,
    bravais_translation_list,
    localized_matrix_element_table,
    unitary_band_mixer,
    quasiparticle_level_offsets,
    displaced_momentum_slot,
    vibration_mode_pulsations,
    occupied_band_tally,
    heat_bath_scale,
):
    kcount = momentum_mesh_positions.shape[1]
    q_local, cells, feat = localized_matrix_element_table.shape
    count, cores = lax.axis_size("ka"), lax.axis_size("pb")
    k_total = kcount * count
    per_q = count // q_local
    me = lax.axis_index("ka")
    tau = heat_bath_scale[0]
    pack = jnp.concatenate(
        [
            unitary_band_mixer,
            quasiparticle_level_offsets,
            momentum_mesh_positions.astype(jnp.bfloat16),
            jnp.broadcast_to(occupied_band_tally.astype(jnp.bfloat16)[:, None], (1, kcount)),
            jnp.zeros((4, kcount), jnp.bfloat16),
        ],
        axis=0,
    )
    q_mine = me // per_q
    slot = lax.dynamic_slice(displaced_momentum_slot, (q_mine, 0), (1, 1))[0, 0]
    shift = jnp.mod(slot - me * kcount, k_total)
    where = jnp.stack([shift, lax.rem(me, per_q) * q_local]).astype(jnp.int32)
    freq_own = vibration_mode_pulsations.astype(jnp.float32)
    freq = lax.dynamic_slice_in_dim(freq_own, q_mine, 1, 0)[0]
    twice = 2.0 / (jnp.exp(freq / tau) - 1.0) + 1.0
    modes = jnp.stack([freq, freq * freq, twice, jnp.broadcast_to(1.0 / tau, (NM,))])
    cell_rows = jnp.pad(bravais_translation_list.astype(jnp.bfloat16), ((0, 0), (8, 5)))

    anywhere = pl.BlockSpec(memory_space=pl.ANY)
    in_vmem = pl.BlockSpec(memory_space=pltpu.VMEM)
    in_smem = pl.BlockSpec(memory_space=pltpu.SMEM)
    packs, part = pl.pallas_call(
        exchange,
        out_shape=(
            jax.ShapeDtypeStruct((count, ROWS, kcount), jnp.bfloat16),
            jax.ShapeDtypeStruct((count, cells, feat), jnp.bfloat16),
        ),
        in_specs=[anywhere] * 2,
        out_specs=(anywhere, anywhere),
        scratch_shapes=[pltpu.SemaphoreType.DMA((count,))] * 4 + [pltpu.SemaphoreType.DMA((2,))],
        compiler_params=pltpu.CompilerParams(collective_id=0, has_side_effects=True),
    )(pack, localized_matrix_element_table)

    sigma, width = pl.pallas_call(
        couple,
        grid=(q_local,),
        out_shape=(
            jax.ShapeDtypeStruct((q_local, NB * 8, 128), jnp.bfloat16),
            jax.ShapeDtypeStruct((8, 128), jnp.float32),
        ),
        in_specs=[in_smem, in_smem, in_vmem, in_vmem, in_vmem],
        out_specs=(
            pl.BlockSpec((1, NB * 8, 128), lambda i: (i, 0, 0)),
            pl.BlockSpec((8, 128), lambda i: (0, 0)),
        ),
        scratch_shapes=[
            pltpu.VMEM((64 * NM * 8, 128), jnp.float32),
            pltpu.VMEM((64 * NM * 8, 128), jnp.bfloat16),
            pltpu.VMEM((16 * 8, 128), jnp.float32),
            pltpu.VMEM((16 * 8, 128), jnp.float32),
            pltpu.VMEM((64 * 16, 128), jnp.bfloat16),
            pltpu.VMEM((64 * 16, 128), jnp.bfloat16),
            pltpu.VMEM((5 * 64, 128), jnp.float32),
            pltpu.VMEM((NB * 8, 128), jnp.float32),
            pltpu.VMEM((NM * 8, 128), jnp.float32),
        ],
        compiler_params=pltpu.CompilerParams(vmem_limit_bytes=48 * 1024 * 1024),
    )(where, modes, packs, part.reshape(count * cells, feat), cell_rows)

    total, widths = pl.pallas_call(
        functools.partial(collect, q_local),
        out_shape=(
            jax.ShapeDtypeStruct((NB * 8, 128), jnp.float32),
            jax.ShapeDtypeStruct((q_local, 8, 128), jnp.float32),
        ),
        in_specs=[in_vmem] * 2,
        out_specs=(in_vmem, in_vmem),
        scratch_shapes=[
            pltpu.VMEM((cores * q_local, NB * 8, 128), jnp.bfloat16),
            pltpu.VMEM((count, 8, 128), jnp.float32),
            pltpu.SemaphoreType.DMA((cores * q_local,)),
            pltpu.SemaphoreType.DMA((cores * q_local,)),
            pltpu.SemaphoreType.DMA((count,)),
            pltpu.SemaphoreType.DMA((count,)),
            pltpu.SemaphoreType.DMA((2,)),
        ],
        compiler_params=pltpu.CompilerParams(collective_id=1, has_side_effects=True),
    )(sigma, width)
    scale = ETA / math.pi
    self_energy = total.reshape(NB, kcount) * (scale / (q_local * cores * NM))
    linewidth = widths[:, 0, :NM] * freq_own * (2.0 * math.pi * scale / k_total)
    return (self_energy, linewidth)


def solution(mesh):
    return jax.shard_map(
        on_device,
        mesh=mesh,
        in_specs=(
            P(None, "ka"),
            P(),
            P(("grp", "pb"), "ka", None),
            P(None, ("grp", "ka")),
            P(None, ("grp", "ka")),
            P(("grp", "pb"), "ka"),
            P(("grp", "pb"), None),
            P(("grp", "ka")),
            P("grp"),
        ),
        out_specs=(P(None, ("grp", "ka")), P(("grp", "pb"), None)),
        check_vma=False,
    )
```

```python
import math

import jax
import jax.numpy as jnp
from jax import lax
from jax.experimental import pallas as pl
from jax.experimental.pallas import tpu as pltpu
from jax.sharding import PartitionSpec as P

NB = 8
NM = 12
ETA = 0.05
TOGETHER = 2
ROWS = 80
MESH = pl.DeviceIdType.MESH
SIN = (6.28318516, -41.3416549, 81.6009982, -76.5496568, 39.5358137)


def fused(
    mode_ref,
    shift_ref,
    u_ref,
    aux_ref,
    table_ref,
    cell_ref,
    energy_ref,
    widths_ref,
    u_all,
    aux_all,
    part,
    flat,
    turned_flat,
    table,
    phase,
    interp,
    near,
    far,
    window,
    level,
    sums,
    acc,
    sigma,
    width,
    got,
    got_w,
    send_aux,
    recv_aux,
    send_part,
    recv_part,
    send_u,
    recv_u,
    send_s,
    recv_s,
    send_w,
    recv_w,
    own_sems,
):
    count = u_all.shape[0]
    q_local = table_ref.shape[0]
    cells = table_ref.shape[1]
    cores = got.shape[0] // q_local
    per_q = count // q_local
    me, core = lax.axis_index("ka"), lax.axis_index("pb")
    q_mine, range_mine = me // per_q, lax.rem(me, per_q)
    slot_mine = core * q_local + q_mine
    everyone = count * cores
    mine = me * cores + core
    barrier = pltpu.get_barrier_semaphore()

    def greet(step, carry):
        other = lax.rem(mine + step, everyone)
        pl.semaphore_signal(
            barrier, inc=1, device_id={"ka": other // cores, "pb": lax.rem(other, cores)}, device_id_type=MESH
        )
        return carry

    lax.fori_loop(1, everyone, greet, 0)
    aux_all[me] = aux_ref[...]
    u_all[me] = u_ref[...]
    own_part = pltpu.make_async_copy(table_ref.at[q_mine], part.at[me], own_sems.at[0])
    own_part.start()
    acc[...] = jnp.zeros_like(acc)
    pl.semaphore_wait(barrier, everyone - 1)

    def to_peer(step, source, target, send, recv, sender):
        return pltpu.make_async_remote_copy(
            src_ref=source,
            dst_ref=target.at[sender],
            send_sem=send.at[step],
            recv_sem=recv.at[sender],
            device_id={"ka": lax.rem(me + step, count)},
            device_id_type=MESH,
        )

    def aux_copy(step, sender):
        return to_peer(step, aux_ref, aux_all, send_aux, recv_aux, sender)

    def part_copy(step, sender):
        return to_peer(step, table_ref.at[lax.rem(me + step, count) // per_q], part, send_part, recv_part, sender)

    def u_copy(step, sender):
        return to_peer(step, u_ref, u_all, send_u, recv_u, sender)

    def width_copy(step, sender):
        return to_peer(step, width, got_w, send_w, recv_w, sender)

    def over_peers(act):
        def body(step, carry):
            act(step, lax.rem(me + step, count))
            return carry

        lax.fori_loop(1, count, body, 0)

    over_peers(lambda step, peer: aux_copy(step, me).start())
    over_peers(lambda step, peer: part_copy(step, me).start())
    over_peers(lambda step, peer: aux_copy(step, peer).wait_recv())

    def phases(b, carry):
        product = jnp.dot(cell_ref[...], aux_all[range_mine * q_local + b], preferred_element_type=jnp.float32)
        turn = product * 0.01
        turn = jnp.abs(turn - jnp.floor(turn + 0.5))
        angle = 0.25 - turn
        square = angle * angle
        value = SIN[4]
        for coefficient in (SIN[3], SIN[2], SIN[1], SIN[0]):
            value = value * square + coefficient
        phase[b] = (value * angle).astype(jnp.bfloat16)
        return carry

    lax.fori_loop(0, q_local, phases, 0)
    own_part.wait()
    over_peers(lambda step, peer: aux_copy(step, me).wait_send())
    over_peers(lambda step, peer: part_copy(step, me).wait_send())
    over_peers(lambda step, peer: u_copy(step, me).start())
    over_peers(lambda step, peer: part_copy(step, peer).wait_recv())

    def flatten(sender, carry):
        flat[pl.ds(pl.multiple_of(sender * cells, cells), cells), :] = part[sender].astype(jnp.float32)
        return carry

    lax.fori_loop(0, count, flatten, 0)
    whole = jnp.transpose(flat[...])
    for j in range(turned_flat.shape[0]):
        turned_flat[j] = whole[:, j * 128 : (j + 1) * 128]
    for v in range(NM):
        for j in range(turned_flat.shape[0]):
            rows = [turned_flat[j, pl.ds(v * 64 + b, 8, stride=8), :] for b in range(NB)]
            table[v * 64 : v * 64 + 64, j * 128 : (j + 1) * 128] = jnp.concatenate(rows, axis=0).astype(jnp.bfloat16)

    def interpolate(b, carry):
        for third in range(3):
            folded = jnp.dot(table[third * 256 : third * 256 + 256, :], phase[b], preferred_element_type=jnp.float32)
            for c in range(8):
                interp[b, pl.ds(third * 2048 + c, 256, stride=8), :] = folded[:, c * 128 : (c + 1) * 128]
        return carry

    lax.fori_loop(0, q_local, interpolate, 0)
    over_peers(lambda step, peer: u_copy(step, me).wait_send())
    over_peers(lambda step, peer: u_copy(step, peer).wait_recv())

    inv_t = mode_ref[3, 0]

    def sigma_copy(index, slot):
        b, to_core = index // cores, lax.rem(index, cores)
        return pltpu.make_async_remote_copy(
            src_ref=sigma.at[b],
            dst_ref=got.at[slot],
            send_sem=send_s.at[index],
            recv_sem=recv_s.at[slot],
            device_id={"ka": range_mine * q_local + b, "pb": to_core},
            device_id_type=MESH,
        )

    def group(ref, start):
        return ref[pl.ds(pl.multiple_of(start, 64), 64), :].reshape(8, 8, 128)

    def fermi(energy):
        return 1.0 / (1.0 + jnp.exp(energy * inv_t))

    def one_block(step, carry):
        b = lax.rem(step + me, q_local)
        block = range_mine * q_local + b
        for c in range(8):
            near[pl.ds(c, 64, stride=8), :] = u_all[block, :, c * 128 : (c + 1) * 128].astype(jnp.float32)
            near[pl.ds(512 + c, 16, stride=8), :] = aux_all[block, :, c * 128 : (c + 1) * 128].astype(jnp.float32)
        for c in range(16):
            lane = pl.ds(c % 8 * 128, 128)

            def chunk(j):
                index = lax.rem(block + c // 8 + j, count)
                rows = aux_all[index, :, lane].astype(jnp.float32)[0:8]
                return jnp.concatenate([u_all[index, :, lane].astype(jnp.float32), rows], axis=0)

            def pick(j, kept):
                wanted = shift_ref[0:1, :] == j.astype(jnp.float32)
                return jnp.where(wanted, chunk(j), kept)

            window[c] = lax.fori_loop(1, count, pick, chunk(0), unroll=count <= 8)
        parts = [window[c] for c in range(12)]
        four = shift_ref[1:2, :] > 0.5
        parts = [jnp.where(four, window[c + 4], parts[c]) for c in range(12)]
        two = shift_ref[2:3, :] > 0.5
        parts = [jnp.where(two, parts[c + 2], parts[c]) for c in range(10)]
        one = shift_ref[3:4, :] > 0.5
        for c in range(9):
            window[c] = jnp.where(one, parts[c + 1], parts[c])
        lanes = lax.broadcasted_iota(jnp.int32, (72, 128), 1).astype(jnp.float32)

        def turned(c):
            rows = window[c]
            for bit in range(7):
                rows = jnp.where(shift_ref[4 + bit : 5 + bit, :] > 0.5, pltpu.roll(rows, 128 - 2**bit, 1), rows)
            return rows

        here = turned(0)
        for c in range(8):
            after = turned(c + 1)
            far[pl.ds(c, 72, stride=8), :] = jnp.where(lanes < 128.0 - shift_ref[11:12, :], here, after)
            here = after

        e_m = group(far, 512)
        f_m = fermi(e_m)
        tally = near[600:608, :]

        def over_n(n, inner_carry):
            e_n = near[pl.ds(pl.multiple_of(512 + n * 8, 8), 8), :]
            f_n = fermi(e_n)
            mask = jnp.where(n.astype(jnp.float32) < tally, 1.0, 0.0)
            gap = e_n[None] - e_m
            level[0] = gap * gap + ETA * ETA
            level[1] = gap + gap
            level[2] = mask[None] * (f_n[None] - f_m)
            level[3] = (1.0 - 2.0 * f_m) * (gap + gap)
            u_n = [near[pl.ds(pl.multiple_of(i * 64 + n * 8, 8), 8), :] for i in range(NB)]

            def over_v(pair, total):
                modes = [pair * TOGETHER + i for i in range(TOGETHER)]
                inner = []
                for v in modes:
                    term = None
                    for i in range(NB):
                        start = pl.multiple_of(v * 512 + i * 64, 64)
                        more = interp[b, pl.ds(start, 64), :].reshape(8, 8, 128) * u_n[i][None]
                        term = more if term is None else term + more
                    inner.append(term)
                rotated = [None] * TOGETHER
                for a in range(NB):
                    u_a = group(far, a * 64)
                    for i in range(TOGETHER):
                        more = u_a * inner[i][a][None]
                        rotated[i] = more if a == 0 else rotated[i] + more
                for i, v in enumerate(modes):
                    w = mode_ref[0, v]
                    even = level[0] + mode_ref[1, v]
                    odd = level[1] * w
                    low = even - odd
                    scaled = rotated[i] * rotated[i] * pl.reciprocal(low * (even + odd), approx=True)
                    total = total + jnp.sum(scaled * (mode_ref[2, v] * even + w * level[3]), axis=0)
                    spot = pl.ds(pl.multiple_of(v * 8, 8), 8)
                    acc[spot, :] = acc[spot, :] + jnp.sum(level[2] * (low * scaled), axis=0)
                return total

            total = lax.fori_loop(0, NM // TOGETHER, over_v, jnp.zeros((8, 128), jnp.float32))
            sums[pl.ds(pl.multiple_of(n * 8, 8), 8), :] = mask * total
            return inner_carry

        lax.fori_loop(0, NB, over_n, 0)
        sigma[b] = sums[...].astype(jnp.bfloat16)
        for to_core in range(cores):

            @pl.when(block * cores + to_core != mine)
            def _():
                sigma_copy(b * cores + to_core, slot_mine).start()

            @pl.when(block * cores + to_core == mine)
            def _():
                got[slot_mine] = sigma[b]

        return carry

    lax.fori_loop(0, q_local, one_block, 0)
    lane = lax.broadcasted_iota(jnp.int32, (8, 128), 1)
    out = jnp.zeros((8, 128), jnp.float32)
    for v in range(NM):
        out = out + jnp.where(lane == v, jnp.sum(acc[v * 8 : v * 8 + 8, :]), 0.0)
    width[...] = out
    got_w[me] = out
    over_peers(lambda step, peer: width_copy(step, me).start())

    def finish_s(index, carry):
        target = (range_mine * q_local + index // cores) * cores + lax.rem(index, cores)

        @pl.when(target != mine)
        def _():
            sigma_copy(index, slot_mine).wait_send()

        from_core, from_q = index // q_local, lax.rem(index, q_local)
        source = (from_q * per_q + me // q_local) * cores + from_core

        @pl.when(source != mine)
        def _():
            sigma_copy(index, index).wait_recv()

        return carry

    lax.fori_loop(0, q_local * cores, finish_s, 0)
    total = got[0].astype(jnp.float32)
    for slot in range(1, q_local * cores):
        total = total + got[slot].astype(jnp.float32)
    sums[...] = total * (ETA / math.pi / (q_local * cores * NM))
    for c in range(8):
        energy_ref[:, c * 128 : (c + 1) * 128] = sums[pl.ds(c, 8, stride=8), :]
    over_peers(lambda step, peer: width_copy(step, me).wait_send())
    over_peers(lambda step, peer: width_copy(step, peer).wait_recv())
    for q in range(q_local):
        total = got_w[q * per_q]
        for part_of in range(1, per_q):
            total = total + got_w[q * per_q + part_of]
        widths_ref[q, :, :] = total


def on_device(
    momentum_mesh_positions,
    bravais_translation_list,
    localized_matrix_element_table,
    unitary_band_mixer,
    quasiparticle_level_offsets,
    displaced_momentum_slot,
    vibration_mode_pulsations,
    occupied_band_tally,
    heat_bath_scale,
):
    kcount = momentum_mesh_positions.shape[1]
    q_local, cells, feat = localized_matrix_element_table.shape
    count, cores = lax.axis_size("ka"), lax.axis_size("pb")
    k_total = kcount * count
    per_q = count // q_local
    me = lax.axis_index("ka")
    tau = heat_bath_scale[0]
    aux = jnp.concatenate(
        [
            quasiparticle_level_offsets,
            momentum_mesh_positions.astype(jnp.bfloat16),
            jnp.broadcast_to(occupied_band_tally.astype(jnp.bfloat16)[:, None], (1, kcount)),
            jnp.zeros((4, kcount), jnp.bfloat16),
        ],
        axis=0,
    )
    q_mine = me // per_q
    slot = lax.dynamic_slice(displaced_momentum_slot, (q_mine, 0), (1, 1))[0, 0]
    shift = jnp.mod(slot - me * kcount, k_total)
    freq_own = vibration_mode_pulsations.astype(jnp.float32)
    freq = lax.dynamic_slice_in_dim(freq_own, q_mine, 1, 0)[0]
    twice = 2.0 / (jnp.exp(freq / tau) - 1.0) + 1.0
    modes = jnp.stack([freq, freq * freq, twice, jnp.broadcast_to(1.0 / tau, (NM,))])
    cell_rows = jnp.pad(bravais_translation_list.astype(jnp.bfloat16), ((0, 0), (8, 5)))

    anywhere = pl.BlockSpec(memory_space=pl.ANY)
    in_vmem = pl.BlockSpec(memory_space=pltpu.VMEM)
    in_smem = pl.BlockSpec(memory_space=pltpu.SMEM)
    inside = shift % kcount
    steps = [shift // kcount, inside // 512, inside // 256 % 2, inside // 128 % 2]
    steps += [inside // 2**bit % 2 for bit in range(7)] + [inside % 128]
    steps = jnp.broadcast_to(jnp.stack(steps + [shift] * 4).astype(jnp.float32)[:, None], (16, 128))
    peers = pltpu.SemaphoreType.DMA((count,))
    slots = pltpu.SemaphoreType.DMA((cores * q_local,))
    self_energy, widths = pl.pallas_call(
        fused,
        out_shape=(
            jax.ShapeDtypeStruct((NB, kcount), jnp.float32),
            jax.ShapeDtypeStruct((q_local, 8, 128), jnp.float32),
        ),
        in_specs=[in_smem, in_vmem, in_vmem, in_vmem, anywhere, in_vmem],
        out_specs=(in_vmem, in_vmem),
        scratch_shapes=[
            pltpu.VMEM((count, 64, kcount), jnp.bfloat16),
            pltpu.VMEM((count, 16, kcount), jnp.bfloat16),
            pltpu.VMEM((count, cells, feat), jnp.bfloat16),
            pltpu.VMEM((count * cells, feat), jnp.float32),
            pltpu.VMEM((count * cells // 128, feat, 128), jnp.float32),
            pltpu.VMEM((feat, count * cells), jnp.bfloat16),
            pltpu.VMEM((q_local, count * cells, kcount), jnp.bfloat16),
            pltpu.VMEM((q_local, feat * 8, 128), jnp.float32),
            pltpu.VMEM((ROWS * 8, 128), jnp.float32),
            pltpu.VMEM((ROWS * 8, 128), jnp.float32),
            pltpu.VMEM((16, 72, 128), jnp.float32),
            pltpu.VMEM((4, NB, 8, 128), jnp.float32),
            pltpu.VMEM((NB * 8, 128), jnp.float32),
            pltpu.VMEM((NM * 8, 128), jnp.float32),
            pltpu.VMEM((q_local, NB * 8, 128), jnp.bfloat16),
            pltpu.VMEM((8, 128), jnp.float32),
            pltpu.VMEM((cores * q_local, NB * 8, 128), jnp.bfloat16),
            pltpu.VMEM((count, 8, 128), jnp.float32),
            peers,
            peers,
            peers,
            peers,
            peers,
            peers,
            slots,
            slots,
            peers,
            peers,
            pltpu.SemaphoreType.DMA((1,)),
        ],
        compiler_params=pltpu.CompilerParams(
            collective_id=0, has_side_effects=True, vmem_limit_bytes=60 * 1024 * 1024
        ),
    )(
        modes,
        steps,
        unitary_band_mixer,
        aux,
        localized_matrix_element_table,
        cell_rows,
    )
    linewidth = widths[:, 0, :NM] * freq_own * (2.0 * math.pi * ETA / math.pi / k_total)
    return (self_energy, linewidth)


def solution(mesh):
    return jax.shard_map(
        on_device,
        mesh=mesh,
        in_specs=(
            P(None, "ka"),
            P(),
            P(("grp", "pb"), "ka", None),
            P(None, ("grp", "ka")),
            P(None, ("grp", "ka")),
            P(("grp", "pb"), "ka"),
            P(("grp", "pb"), None),
            P(("grp", "ka")),
            P("grp"),
        ),
        out_specs=(P(None, ("grp", "ka")), P(("grp", "pb"), None)),
        check_vma=False,
    )
```

```python
import math

import jax
import jax.numpy as jnp
from jax import lax
from jax.experimental import pallas as pl
from jax.experimental.pallas import tpu as pltpu
from jax.sharding import PartitionSpec as P

NB = 8
NM = 12
ETA = 0.05
TOGETHER = 3
ROWS = 80
MESH = pl.DeviceIdType.MESH
SIN = (6.28318516, -41.3416549, 81.6009982, -76.5496568, 39.5358137)


def fused(
    mode_ref,
    shift_ref,
    u_ref,
    aux_ref,
    table_ref,
    cell_ref,
    freq_ref,
    energy_ref,
    widths_ref,
    u_all,
    aux_all,
    part,
    flat,
    turned_flat,
    table,
    phase,
    interp,
    near,
    far,
    window,
    level,
    sums,
    acc,
    sigma,
    width,
    got,
    got_w,
    send_aux,
    recv_aux,
    send_part,
    recv_part,
    send_u,
    recv_u,
    send_f,
    recv_f,
    send_s,
    recv_s,
    send_w,
    recv_w,
    own_sems,
):
    count = u_all.shape[0]
    q_local = table_ref.shape[0]
    cells = table_ref.shape[1]
    cores = got.shape[0] // q_local
    per_q = count // q_local
    me, core = lax.axis_index("ka"), lax.axis_index("pb")
    q_mine, range_mine = me // per_q, lax.rem(me, per_q)
    slot_mine = core * q_local + q_mine
    everyone = count * cores
    mine = me * cores + core
    barrier = pltpu.get_barrier_semaphore()

    def greet(step, carry):
        other = lax.rem(mine + step, everyone)
        pl.semaphore_signal(
            barrier, inc=1, device_id={"ka": other // cores, "pb": lax.rem(other, cores)}, device_id_type=MESH
        )
        return carry

    lax.fori_loop(1, everyone, greet, 0)
    aux_all[me] = aux_ref[...]
    u_all[me] = u_ref[...]
    own_part = pltpu.make_async_copy(table_ref.at[q_mine], part.at[me], own_sems.at[0])
    own_part.start()
    acc[...] = jnp.zeros_like(acc)
    pl.semaphore_wait(barrier, everyone - 1)

    def to_peer(step, source, target, send, recv, sender):
        return pltpu.make_async_remote_copy(
            src_ref=source,
            dst_ref=target.at[sender],
            send_sem=send.at[step],
            recv_sem=recv.at[sender],
            device_id={"ka": lax.rem(me + step, count)},
            device_id_type=MESH,
        )

    def aux_copy(step, sender):
        return to_peer(step, aux_ref, aux_all, send_aux, recv_aux, sender)

    def part_copy(step, sender):
        return to_peer(step, table_ref.at[lax.rem(me + step, count) // per_q], part, send_part, recv_part, sender)

    half = u_ref.shape[1] // cores

    def u_copy(step, sender):
        columns = pl.ds(pl.multiple_of(core * half, half), half)
        return pltpu.make_async_remote_copy(
            src_ref=u_ref.at[:, columns],
            dst_ref=u_all.at[sender, :, columns],
            send_sem=send_u.at[step],
            recv_sem=recv_u.at[sender],
            device_id={"ka": lax.rem(me + step, count)},
            device_id_type=MESH,
        )

    def pass_on(sender, from_core):
        columns = pl.ds(pl.multiple_of(from_core * half, half), half)
        return pltpu.make_async_remote_copy(
            src_ref=u_all.at[sender, :, columns],
            dst_ref=u_all.at[sender, :, columns],
            send_sem=send_f.at[sender],
            recv_sem=recv_f.at[sender],
            device_id={"pb": 1 - core},
            device_id_type=MESH,
        )

    def width_copy(step, sender):
        return to_peer(step, width, got_w, send_w, recv_w, sender)

    def over_peers(act):
        def body(step, carry):
            act(step, lax.rem(me + step, count))
            return carry

        lax.fori_loop(1, count, body, 0)

    over_peers(lambda step, peer: aux_copy(step, me).start())
    over_peers(lambda step, peer: part_copy(step, me).start())
    over_peers(lambda step, peer: aux_copy(step, peer).wait_recv())

    def phases(b, carry):
        product = jnp.dot(cell_ref[...], aux_all[range_mine * q_local + b], preferred_element_type=jnp.float32)
        turn = product * 0.01
        turn = jnp.abs(turn - jnp.floor(turn + 0.5))
        angle = 0.25 - turn
        square = angle * angle
        value = SIN[4]
        for coefficient in (SIN[3], SIN[2], SIN[1], SIN[0]):
            value = value * square + coefficient
        phase[b] = (value * angle).astype(jnp.bfloat16)
        return carry

    lax.fori_loop(0, q_local, phases, 0)
    own_part.wait()
    over_peers(lambda step, peer: aux_copy(step, me).wait_send())
    over_peers(lambda step, peer: part_copy(step, me).wait_send())
    over_peers(lambda step, peer: u_copy(step, me).start())
    over_peers(lambda step, peer: part_copy(step, peer).wait_recv())

    def flatten(sender, carry):
        flat[pl.ds(pl.multiple_of(sender * cells, cells), cells), :] = part[sender].astype(jnp.float32)
        return carry

    lax.fori_loop(0, count, flatten, 0)
    whole = jnp.transpose(flat[...])
    for j in range(turned_flat.shape[0]):
        turned_flat[j] = whole[:, j * 128 : (j + 1) * 128]
    for v in range(NM):
        for j in range(turned_flat.shape[0]):
            rows = [turned_flat[j, pl.ds(v * 64 + b, 8, stride=8), :] for b in range(NB)]
            table[v * 64 : v * 64 + 64, j * 128 : (j + 1) * 128] = jnp.concatenate(rows, axis=0).astype(jnp.bfloat16)

    def interpolate(b, carry):
        folded = jnp.dot(table[...], phase[b], preferred_element_type=jnp.float32)
        for c in range(8):
            interp[b, pl.ds(c, 64 * NM, stride=8), :] = folded[:, c * 128 : (c + 1) * 128]

        def relay(step, inner_carry):
            peer = lax.rem(me + step, count)
            u_copy(step, peer).wait_recv()
            pass_on(peer, core).start()
            return inner_carry

        batch = count // (q_local // 2)
        late = b - q_local // 2
        lax.fori_loop(jnp.maximum(late * batch, 1), (late + 1) * batch, relay, 0)
        return carry

    lax.fori_loop(0, q_local, interpolate, 0)
    over_peers(lambda step, peer: u_copy(step, me).wait_send())
    over_peers(lambda step, peer: pass_on(peer, core).wait_send())
    over_peers(lambda step, peer: pass_on(peer, 1 - core).wait_recv())

    inv_t = mode_ref[3, 0]

    def sigma_copy(index, slot):
        b, to_core = index // cores, lax.rem(index, cores)
        return pltpu.make_async_remote_copy(
            src_ref=sigma.at[b],
            dst_ref=got.at[slot],
            send_sem=send_s.at[index],
            recv_sem=recv_s.at[slot],
            device_id={"ka": range_mine * q_local + b, "pb": to_core},
            device_id_type=MESH,
        )

    def group(ref, start):
        return ref[pl.ds(pl.multiple_of(start, 64), 64), :].reshape(8, 8, 128)

    def fermi(energy):
        return 1.0 / (1.0 + jnp.exp(energy * inv_t))

    def one_block(step, carry):
        b = lax.rem(step + me, q_local)
        block = range_mine * q_local + b
        for c in range(8):
            near[pl.ds(c, 64, stride=8), :] = u_all[block, :, c * 128 : (c + 1) * 128].astype(jnp.float32)
            near[pl.ds(512 + c, 16, stride=8), :] = aux_all[block, :, c * 128 : (c + 1) * 128].astype(jnp.float32)
        for c in range(16):
            lane = pl.ds(c % 8 * 128, 128)

            def chunk(j):
                index = lax.rem(block + c // 8 + j, count)
                rows = aux_all[index, :, lane].astype(jnp.float32)[0:8]
                return jnp.concatenate([u_all[index, :, lane].astype(jnp.float32), rows], axis=0)

            def pick(j, kept):
                wanted = shift_ref[0:1, :] == j.astype(jnp.float32)
                return jnp.where(wanted, chunk(j), kept)

            window[c] = lax.fori_loop(1, count, pick, chunk(0), unroll=count <= 8)
        parts = [window[c] for c in range(12)]
        four = shift_ref[1:2, :] > 0.5
        parts = [jnp.where(four, window[c + 4], parts[c]) for c in range(12)]
        two = shift_ref[2:3, :] > 0.5
        parts = [jnp.where(two, parts[c + 2], parts[c]) for c in range(10)]
        one = shift_ref[3:4, :] > 0.5
        for c in range(9):
            window[c] = jnp.where(one, parts[c + 1], parts[c])
        lanes = lax.broadcasted_iota(jnp.int32, (72, 128), 1).astype(jnp.float32)

        def turned(c):
            rows = window[c]
            for bit in range(7):
                rows = jnp.where(shift_ref[4 + bit : 5 + bit, :] > 0.5, pltpu.roll(rows, 128 - 2**bit, 1), rows)
            return rows

        here = turned(0)
        for c in range(8):
            after = turned(c + 1)
            far[pl.ds(c, 72, stride=8), :] = jnp.where(lanes < 128.0 - shift_ref[11:12, :], here, after)
            here = after

        e_m = group(far, 512)
        f_m = fermi(e_m)
        tally = near[600:608, :]

        def over_n(n, inner_carry):
            e_n = near[pl.ds(pl.multiple_of(512 + n * 8, 8), 8), :]
            f_n = fermi(e_n)
            mask = jnp.where(n.astype(jnp.float32) < tally, 1.0, 0.0)
            gap = e_n[None] - e_m
            level[0] = gap * gap + ETA * ETA
            level[1] = gap + gap
            level[2] = mask[None] * (f_n[None] - f_m)
            level[3] = (1.0 - 2.0 * f_m) * (gap + gap)
            u_n = [near[pl.ds(pl.multiple_of(i * 64 + n * 8, 8), 8), :] for i in range(NB)]

            def over_v(pair, total):
                modes = [pair * TOGETHER + i for i in range(TOGETHER)]
                inner = []
                for v in modes:
                    term = None
                    for i in range(NB):
                        start = pl.multiple_of(v * 512 + i * 64, 64)
                        more = interp[b, pl.ds(start, 64), :].reshape(8, 8, 128) * u_n[i][None]
                        term = more if term is None else term + more
                    inner.append(term)
                rotated = [None] * TOGETHER
                for a in range(NB):
                    u_a = group(far, a * 64)
                    for i in range(TOGETHER):
                        more = u_a * inner[i][a][None]
                        rotated[i] = more if a == 0 else rotated[i] + more
                for i, v in enumerate(modes):
                    w = mode_ref[0, v]
                    even = level[0] + mode_ref[1, v]
                    odd = level[1] * w
                    low = even - odd
                    scaled = rotated[i] * rotated[i] * pl.reciprocal(low * (even + odd), approx=True)
                    total = total + jnp.sum(scaled * (mode_ref[2, v] * even + w * level[3]), axis=0)
                    spot = pl.ds(pl.multiple_of(v * 8, 8), 8)
                    acc[spot, :] = acc[spot, :] + jnp.sum(level[2] * (low * scaled), axis=0)
                return total

            total = lax.fori_loop(0, NM // TOGETHER, over_v, jnp.zeros((8, 128), jnp.float32))
            sums[pl.ds(pl.multiple_of(n * 8, 8), 8), :] = mask * total
            return inner_carry

        lax.fori_loop(0, NB, over_n, 0)
        sigma[b] = sums[...].astype(jnp.bfloat16)
        for to_core in range(cores):

            @pl.when(block * cores + to_core != mine)
            def _():
                sigma_copy(b * cores + to_core, slot_mine).start()

            @pl.when(block * cores + to_core == mine)
            def _():
                got[slot_mine] = sigma[b]

        return carry

    lax.fori_loop(0, q_local, one_block, 0)
    lane = lax.broadcasted_iota(jnp.int32, (8, 128), 1)
    out = jnp.zeros((8, 128), jnp.float32)
    for v in range(NM):
        out = out + jnp.where(lane == v, jnp.sum(acc[v * 8 : v * 8 + 8, :]), 0.0)
    width[...] = out
    got_w[me] = out
    over_peers(lambda step, peer: width_copy(step, me).start())

    def finish_s(index, carry):
        target = (range_mine * q_local + index // cores) * cores + lax.rem(index, cores)

        @pl.when(target != mine)
        def _():
            sigma_copy(index, slot_mine).wait_send()

        from_core, from_q = index // q_local, lax.rem(index, q_local)
        source = (from_q * per_q + me // q_local) * cores + from_core

        @pl.when(source != mine)
        def _():
            sigma_copy(index, index).wait_recv()

        return carry

    lax.fori_loop(0, q_local * cores, finish_s, 0)
    total = got[0].astype(jnp.float32)
    for slot in range(1, q_local * cores):
        total = total + got[slot].astype(jnp.float32)
    sums[...] = total * (ETA / math.pi / (q_local * cores * NM))
    for c in range(8):
        energy_ref[:, c * 128 : (c + 1) * 128] = sums[pl.ds(c, 8, stride=8), :]
    over_peers(lambda step, peer: width_copy(step, me).wait_send())
    over_peers(lambda step, peer: width_copy(step, peer).wait_recv())
    for q in range(q_local):
        total = got_w[q * per_q]
        for part_of in range(1, per_q):
            total = total + got_w[q * per_q + part_of]
        widths_ref[q : q + 1, :] = total[0:1, :NM] * freq_ref[q : q + 1, :] * (2.0 * ETA / (count * u_ref.shape[1]))


def on_device(
    momentum_mesh_positions,
    bravais_translation_list,
    localized_matrix_element_table,
    unitary_band_mixer,
    quasiparticle_level_offsets,
    displaced_momentum_slot,
    vibration_mode_pulsations,
    occupied_band_tally,
    heat_bath_scale,
):
    kcount = momentum_mesh_positions.shape[1]
    q_local, cells, feat = localized_matrix_element_table.shape
    count, cores = lax.axis_size("ka"), lax.axis_size("pb")
    k_total = kcount * count
    per_q = count // q_local
    me = lax.axis_index("ka")
    tau = heat_bath_scale[0]
    aux = jnp.concatenate(
        [
            quasiparticle_level_offsets,
            momentum_mesh_positions.astype(jnp.bfloat16),
            jnp.broadcast_to(occupied_band_tally.astype(jnp.bfloat16)[:, None], (1, kcount)),
            jnp.zeros((4, kcount), jnp.bfloat16),
        ],
        axis=0,
    )
    q_mine = me // per_q
    slot = lax.dynamic_slice(displaced_momentum_slot, (q_mine, 0), (1, 1))[0, 0]
    shift = jnp.mod(slot - me * kcount, k_total)
    freq_own = vibration_mode_pulsations.astype(jnp.float32)
    freq = lax.dynamic_slice_in_dim(freq_own, q_mine, 1, 0)[0]
    twice = 2.0 / (jnp.exp(freq / tau) - 1.0) + 1.0
    modes = jnp.stack([freq, freq * freq, twice, jnp.broadcast_to(1.0 / tau, (NM,))])
    cell_rows = jnp.pad(bravais_translation_list.astype(jnp.bfloat16), ((0, 0), (8, 5)))

    anywhere = pl.BlockSpec(memory_space=pl.ANY)
    in_vmem = pl.BlockSpec(memory_space=pltpu.VMEM)
    in_smem = pl.BlockSpec(memory_space=pltpu.SMEM)
    inside = shift % kcount
    steps = [shift // kcount, inside // 512, inside // 256 % 2, inside // 128 % 2]
    steps += [inside // 2**bit % 2 for bit in range(7)] + [inside % 128]
    steps = jnp.broadcast_to(jnp.stack(steps + [shift] * 4).astype(jnp.float32)[:, None], (16, 128))
    peers = pltpu.SemaphoreType.DMA((count,))
    slots = pltpu.SemaphoreType.DMA((cores * q_local,))
    self_energy, linewidth = pl.pallas_call(
        fused,
        out_shape=(
            jax.ShapeDtypeStruct((NB, kcount), jnp.float32),
            jax.ShapeDtypeStruct((q_local, NM), jnp.float32),
        ),
        in_specs=[in_smem, in_vmem, in_vmem, in_vmem, anywhere, in_vmem, in_vmem],
        out_specs=(in_vmem, in_vmem),
        scratch_shapes=[
            pltpu.VMEM((count, 64, kcount), jnp.bfloat16),
            pltpu.VMEM((count, 16, kcount), jnp.bfloat16),
            pltpu.VMEM((count, cells, feat), jnp.bfloat16),
            pltpu.VMEM((count * cells, feat), jnp.float32),
            pltpu.VMEM((count * cells // 128, feat, 128), jnp.float32),
            pltpu.VMEM((feat, count * cells), jnp.bfloat16),
            pltpu.VMEM((q_local, count * cells, kcount), jnp.bfloat16),
            pltpu.VMEM((q_local, feat * 8, 128), jnp.float32),
            pltpu.VMEM((ROWS * 8, 128), jnp.float32),
            pltpu.VMEM((ROWS * 8, 128), jnp.float32),
            pltpu.VMEM((16, 72, 128), jnp.float32),
            pltpu.VMEM((4, NB, 8, 128), jnp.float32),
            pltpu.VMEM((NB * 8, 128), jnp.float32),
            pltpu.VMEM((NM * 8, 128), jnp.float32),
            pltpu.VMEM((q_local, NB * 8, 128), jnp.bfloat16),
            pltpu.VMEM((8, 128), jnp.float32),
            pltpu.VMEM((cores * q_local, NB * 8, 128), jnp.bfloat16),
            pltpu.VMEM((count, 8, 128), jnp.float32),
            peers,
            peers,
            peers,
            peers,
            peers,
            peers,
            peers,
            peers,
            slots,
            slots,
            peers,
            peers,
            pltpu.SemaphoreType.DMA((1,)),
        ],
        compiler_params=pltpu.CompilerParams(
            collective_id=0, has_side_effects=True, vmem_limit_bytes=60 * 1024 * 1024
        ),
    )(
        modes,
        steps,
        unitary_band_mixer,
        aux,
        localized_matrix_element_table,
        cell_rows,
        freq_own,
    )
    return (self_energy, linewidth)


def solution(mesh):
    return jax.shard_map(
        on_device,
        mesh=mesh,
        in_specs=(
            P(None, "ka"),
            P(),
            P(("grp", "pb"), "ka", None),
            P(None, ("grp", "ka")),
            P(None, ("grp", "ka")),
            P(("grp", "pb"), "ka"),
            P(("grp", "pb"), None),
            P(("grp", "ka")),
            P("grp"),
        ),
        out_specs=(P(None, ("grp", "ka")), P(("grp", "pb"), None)),
        check_vma=False,
    )
```

```python
import math

import jax
import jax.numpy as jnp
from jax import lax
from jax.experimental import pallas as pl
from jax.experimental.pallas import tpu as pltpu
from jax.sharding import PartitionSpec as P

NB = 8
NM = 12
ETA = 0.05
TOGETHER = 3
ROWS = 80
MESH = pl.DeviceIdType.MESH
SIN = (6.28318516, -41.3416549, 81.6009982, -76.5496568, 39.5358137)


def fused(
    mode_ref,
    shift_ref,
    u_ref,
    aux_ref,
    table_ref,
    cell_ref,
    freq_ref,
    energy_ref,
    widths_ref,
    u_all,
    aux_all,
    part,
    flat,
    turned_flat,
    table,
    phase,
    interp,
    near,
    far,
    raw,
    window,
    level,
    sums,
    acc,
    sigma,
    width,
    got,
    got_w,
    send_aux,
    recv_aux,
    send_part,
    recv_part,
    send_u,
    recv_u,
    send_f,
    recv_f,
    send_s,
    recv_s,
    send_w,
    recv_w,
    own_sems,
):
    count = u_all.shape[0]
    q_local = table_ref.shape[0]
    cells = table_ref.shape[1]
    cores = got.shape[0] // q_local
    per_q = count // q_local
    me, core = lax.axis_index("ka"), lax.axis_index("pb")
    q_mine, range_mine = me // per_q, lax.rem(me, per_q)
    slot_mine = core * q_local + q_mine
    everyone = count * cores
    mine = me * cores + core
    barrier = pltpu.get_barrier_semaphore()

    def greet(step, carry):
        other = lax.rem(mine + step, everyone)
        pl.semaphore_signal(
            barrier, inc=1, device_id={"ka": other // cores, "pb": lax.rem(other, cores)}, device_id_type=MESH
        )
        return carry

    lax.fori_loop(1, everyone, greet, 0)
    aux_all[me] = aux_ref[...]
    u_all[me] = u_ref[...]
    own_part = pltpu.make_async_copy(table_ref.at[q_mine], part.at[me], own_sems.at[0])
    own_part.start()
    acc[...] = jnp.zeros_like(acc)
    pl.semaphore_wait(barrier, everyone - 1)

    def to_peer(step, source, target, send, recv, sender):
        return pltpu.make_async_remote_copy(
            src_ref=source,
            dst_ref=target.at[sender],
            send_sem=send.at[step],
            recv_sem=recv.at[sender],
            device_id={"ka": lax.rem(me + step, count)},
            device_id_type=MESH,
        )

    def aux_copy(step, sender):
        return to_peer(step, aux_ref, aux_all, send_aux, recv_aux, sender)

    def part_copy(step, sender):
        return to_peer(step, table_ref.at[lax.rem(me + step, count) // per_q], part, send_part, recv_part, sender)

    half = u_ref.shape[1] // cores

    def u_copy(step, sender):
        columns = pl.ds(pl.multiple_of(core * half, half), half)
        return pltpu.make_async_remote_copy(
            src_ref=u_ref.at[:, columns],
            dst_ref=u_all.at[sender, :, columns],
            send_sem=send_u.at[step],
            recv_sem=recv_u.at[sender],
            device_id={"ka": lax.rem(me + step, count)},
            device_id_type=MESH,
        )

    def pass_on(sender, from_core):
        columns = pl.ds(pl.multiple_of(from_core * half, half), half)
        return pltpu.make_async_remote_copy(
            src_ref=u_all.at[sender, :, columns],
            dst_ref=u_all.at[sender, :, columns],
            send_sem=send_f.at[sender],
            recv_sem=recv_f.at[sender],
            device_id={"pb": 1 - core},
            device_id_type=MESH,
        )

    def width_copy(step, sender):
        return to_peer(step, width, got_w, send_w, recv_w, sender)

    def over_peers(act):
        def body(step, carry):
            act(step, lax.rem(me + step, count))
            return carry

        lax.fori_loop(1, count, body, 0)

    over_peers(lambda step, peer: aux_copy(step, me).start())
    over_peers(lambda step, peer: part_copy(step, me).start())
    over_peers(lambda step, peer: aux_copy(step, peer).wait_recv())

    def phases(b, carry):
        product = jnp.dot(cell_ref[...], aux_all[range_mine * q_local + b], preferred_element_type=jnp.float32)
        turn = product * 0.01
        turn = jnp.abs(turn - jnp.floor(turn + 0.5))
        angle = 0.25 - turn
        square = angle * angle
        value = SIN[4]
        for coefficient in (SIN[3], SIN[2], SIN[1], SIN[0]):
            value = value * square + coefficient
        phase[b] = (value * angle).astype(jnp.bfloat16)
        return carry

    lax.fori_loop(0, q_local, phases, 0)
    own_part.wait()
    over_peers(lambda step, peer: aux_copy(step, me).wait_send())
    over_peers(lambda step, peer: part_copy(step, me).wait_send())
    over_peers(lambda step, peer: u_copy(step, me).start())
    over_peers(lambda step, peer: part_copy(step, peer).wait_recv())

    def flatten(sender, carry):
        flat[pl.ds(pl.multiple_of(sender * cells, cells), cells), :] = part[sender].astype(jnp.float32)
        return carry

    lax.fori_loop(0, count, flatten, 0)
    whole = jnp.transpose(flat[...])
    for j in range(turned_flat.shape[0]):
        turned_flat[j] = whole[:, j * 128 : (j + 1) * 128]
    for v in range(NM):
        for j in range(turned_flat.shape[0]):
            rows = [turned_flat[j, pl.ds(v * 64 + b, 8, stride=8), :] for b in range(NB)]
            table[v * 64 : v * 64 + 64, j * 128 : (j + 1) * 128] = jnp.concatenate(rows, axis=0).astype(jnp.bfloat16)

    def interpolate(b, carry):
        folded = jnp.dot(table[...], phase[b], preferred_element_type=jnp.float32)
        for c in range(8):
            interp[b, pl.ds(c, 64 * NM, stride=8), :] = folded[:, c * 128 : (c + 1) * 128]

        def relay(step, inner_carry):
            peer = lax.rem(me + step, count)
            u_copy(step, peer).wait_recv()
            pass_on(peer, core).start()
            return inner_carry

        batch = count // (q_local // 2)
        late = b - q_local // 2
        lax.fori_loop(jnp.maximum(late * batch, 1), (late + 1) * batch, relay, 0)
        return carry

    lax.fori_loop(0, q_local, interpolate, 0)
    over_peers(lambda step, peer: u_copy(step, me).wait_send())
    over_peers(lambda step, peer: pass_on(peer, core).wait_send())
    over_peers(lambda step, peer: pass_on(peer, 1 - core).wait_recv())

    inv_t = mode_ref[3, 0]

    def sigma_copy(index, slot):
        b, to_core = index // cores, lax.rem(index, cores)
        return pltpu.make_async_remote_copy(
            src_ref=sigma.at[b],
            dst_ref=got.at[slot],
            send_sem=send_s.at[index],
            recv_sem=recv_s.at[slot],
            device_id={"ka": range_mine * q_local + b, "pb": to_core},
            device_id_type=MESH,
        )

    def group(ref, start):
        return ref[pl.ds(pl.multiple_of(start, 64), 64), :].reshape(8, 8, 128)

    def fermi(energy):
        return 1.0 / (1.0 + jnp.exp(energy * inv_t))

    def fetch(block):
        for c in range(8):
            lane = pl.ds(c * 128, 128)

            def chunk(j):
                index = lax.rem(block + j, count)
                rows = aux_all[index, :, lane].astype(jnp.float32)[0:8]
                return jnp.concatenate([u_all[index, :, lane].astype(jnp.float32), rows], axis=0)

            def pick(j, kept):
                wanted = shift_ref[0:1, :] == j.astype(jnp.float32)
                return jnp.where(wanted, chunk(j), kept)

            raw[8 + c] = lax.fori_loop(1, count, pick, chunk(0), unroll=count <= 8)

    fetch(range_mine * q_local)

    def one_block(b, carry):
        block = range_mine * q_local + b
        for c in range(8):
            near[pl.ds(c, 64, stride=8), :] = u_all[block, :, c * 128 : (c + 1) * 128].astype(jnp.float32)
            near[pl.ds(512 + c, 16, stride=8), :] = aux_all[block, :, c * 128 : (c + 1) * 128].astype(jnp.float32)
        for c in range(8):
            raw[c] = raw[8 + c]
        fetch(block + 1)
        parts = [raw[c] for c in range(12)]
        four = shift_ref[1:2, :] > 0.5
        parts = [jnp.where(four, raw[c + 4], parts[c]) for c in range(12)]
        two = shift_ref[2:3, :] > 0.5
        parts = [jnp.where(two, parts[c + 2], parts[c]) for c in range(10)]
        one = shift_ref[3:4, :] > 0.5
        for c in range(9):
            window[c] = jnp.where(one, parts[c + 1], parts[c])
        lanes = lax.broadcasted_iota(jnp.int32, (72, 128), 1).astype(jnp.float32)

        def turned(c):
            rows = window[c]
            for bit in range(7):
                rows = jnp.where(shift_ref[4 + bit : 5 + bit, :] > 0.5, pltpu.roll(rows, 128 - 2**bit, 1), rows)
            return rows

        here = turned(0)
        for c in range(8):
            after = turned(c + 1)
            far[pl.ds(c, 72, stride=8), :] = jnp.where(lanes < 128.0 - shift_ref[11:12, :], here, after)
            here = after

        e_m = group(far, 512)
        f_m = fermi(e_m)
        tally = near[600:608, :]

        def over_n(n, inner_carry):
            e_n = near[pl.ds(pl.multiple_of(512 + n * 8, 8), 8), :]
            f_n = fermi(e_n)
            mask = jnp.where(n.astype(jnp.float32) < tally, 1.0, 0.0)
            gap = e_n[None] - e_m
            level[0] = gap * gap + ETA * ETA
            level[1] = gap + gap
            level[2] = mask[None] * (f_n[None] - f_m)
            level[3] = (1.0 - 2.0 * f_m) * (gap + gap)
            u_n = [near[pl.ds(pl.multiple_of(i * 64 + n * 8, 8), 8), :] for i in range(NB)]

            def over_v(pair, total):
                modes = [pair * TOGETHER + i for i in range(TOGETHER)]
                inner = []
                for v in modes:
                    term = None
                    for i in range(NB):
                        start = pl.multiple_of(v * 512 + i * 64, 64)
                        more = interp[b, pl.ds(start, 64), :].reshape(8, 8, 128) * u_n[i][None]
                        term = more if term is None else term + more
                    inner.append(term)
                rotated = [None] * TOGETHER
                for a in range(NB):
                    u_a = group(far, a * 64)
                    for i in range(TOGETHER):
                        more = u_a * inner[i][a][None]
                        rotated[i] = more if a == 0 else rotated[i] + more
                for i, v in enumerate(modes):
                    w = mode_ref[0, v]
                    even = level[0] + mode_ref[1, v]
                    odd = level[1] * w
                    low = even - odd
                    scaled = rotated[i] * rotated[i] * pl.reciprocal(low * (even + odd), approx=True)
                    total = total + jnp.sum(scaled * (mode_ref[2, v] * even + w * level[3]), axis=0)
                    spot = pl.ds(pl.multiple_of(v * 8, 8), 8)
                    acc[spot, :] = acc[spot, :] + jnp.sum(level[2] * (low * scaled), axis=0)
                return total

            total = lax.fori_loop(0, NM // TOGETHER, over_v, jnp.zeros((8, 128), jnp.float32))
            sums[pl.ds(pl.multiple_of(n * 8, 8), 8), :] = mask * total
            return inner_carry

        lax.fori_loop(0, NB, over_n, 0)
        sigma[b] = sums[...].astype(jnp.bfloat16)
        for to_core in range(cores):

            @pl.when(block * cores + to_core != mine)
            def _():
                sigma_copy(b * cores + to_core, slot_mine).start()

            @pl.when(block * cores + to_core == mine)
            def _():
                got[slot_mine] = sigma[b]

        return carry

    lax.fori_loop(0, q_local, one_block, 0)
    lane = lax.broadcasted_iota(jnp.int32, (8, 128), 1)
    out = jnp.zeros((8, 128), jnp.float32)
    for v in range(NM):
        out = out + jnp.where(lane == v, jnp.sum(acc[v * 8 : v * 8 + 8, :]), 0.0)
    width[...] = out
    got_w[me] = out
    over_peers(lambda step, peer: width_copy(step, me).start())

    def finish_s(index, carry):
        target = (range_mine * q_local + index // cores) * cores + lax.rem(index, cores)

        @pl.when(target != mine)
        def _():
            sigma_copy(index, slot_mine).wait_send()

        from_core, from_q = index // q_local, lax.rem(index, q_local)
        source = (from_q * per_q + me // q_local) * cores + from_core

        @pl.when(source != mine)
        def _():
            sigma_copy(index, index).wait_recv()

        return carry

    lax.fori_loop(0, q_local * cores, finish_s, 0)
    total = got[0].astype(jnp.float32)
    for slot in range(1, q_local * cores):
        total = total + got[slot].astype(jnp.float32)
    sums[...] = total * (ETA / math.pi / (q_local * cores * NM))
    for c in range(8):
        energy_ref[:, c * 128 : (c + 1) * 128] = sums[pl.ds(c, 8, stride=8), :]
    over_peers(lambda step, peer: width_copy(step, me).wait_send())
    over_peers(lambda step, peer: width_copy(step, peer).wait_recv())
    for q in range(q_local):
        total = got_w[q * per_q]
        for part_of in range(1, per_q):
            total = total + got_w[q * per_q + part_of]
        widths_ref[q : q + 1, :] = total[0:1, :NM] * freq_ref[q : q + 1, :] * (2.0 * ETA / (count * u_ref.shape[1]))


def on_device(
    momentum_mesh_positions,
    bravais_translation_list,
    localized_matrix_element_table,
    unitary_band_mixer,
    quasiparticle_level_offsets,
    displaced_momentum_slot,
    vibration_mode_pulsations,
    occupied_band_tally,
    heat_bath_scale,
):
    kcount = momentum_mesh_positions.shape[1]
    q_local, cells, feat = localized_matrix_element_table.shape
    count, cores = lax.axis_size("ka"), lax.axis_size("pb")
    k_total = kcount * count
    per_q = count // q_local
    me = lax.axis_index("ka")
    tau = heat_bath_scale[0]
    aux = jnp.concatenate(
        [
            quasiparticle_level_offsets,
            momentum_mesh_positions.astype(jnp.bfloat16),
            jnp.broadcast_to(occupied_band_tally.astype(jnp.bfloat16)[:, None], (1, kcount)),
            jnp.zeros((4, kcount), jnp.bfloat16),
        ],
        axis=0,
    )
    q_mine = me // per_q
    slot = lax.dynamic_slice(displaced_momentum_slot, (q_mine, 0), (1, 1))[0, 0]
    shift = jnp.mod(slot - me * kcount, k_total)
    freq_own = vibration_mode_pulsations.astype(jnp.float32)
    freq = lax.dynamic_slice_in_dim(freq_own, q_mine, 1, 0)[0]
    twice = 2.0 / (jnp.exp(freq / tau) - 1.0) + 1.0
    modes = jnp.stack([freq, freq * freq, twice, jnp.broadcast_to(1.0 / tau, (NM,))])
    cell_rows = jnp.pad(bravais_translation_list.astype(jnp.bfloat16), ((0, 0), (8, 5)))

    anywhere = pl.BlockSpec(memory_space=pl.ANY)
    in_vmem = pl.BlockSpec(memory_space=pltpu.VMEM)
    in_smem = pl.BlockSpec(memory_space=pltpu.SMEM)
    inside = shift % kcount
    steps = [shift // kcount, inside // 512, inside // 256 % 2, inside // 128 % 2]
    steps += [inside // 2**bit % 2 for bit in range(7)] + [inside % 128]
    steps = jnp.broadcast_to(jnp.stack(steps + [shift] * 4).astype(jnp.float32)[:, None], (16, 128))
    peers = pltpu.SemaphoreType.DMA((count,))
    slots = pltpu.SemaphoreType.DMA((cores * q_local,))
    self_energy, linewidth = pl.pallas_call(
        fused,
        out_shape=(
            jax.ShapeDtypeStruct((NB, kcount), jnp.float32),
            jax.ShapeDtypeStruct((q_local, NM), jnp.float32),
        ),
        in_specs=[in_smem, in_vmem, in_vmem, in_vmem, anywhere, in_vmem, in_vmem],
        out_specs=(in_vmem, in_vmem),
        scratch_shapes=[
            pltpu.VMEM((count, 64, kcount), jnp.bfloat16),
            pltpu.VMEM((count, 16, kcount), jnp.bfloat16),
            pltpu.VMEM((count, cells, feat), jnp.bfloat16),
            pltpu.VMEM((count * cells, feat), jnp.float32),
            pltpu.VMEM((count * cells // 128, feat, 128), jnp.float32),
            pltpu.VMEM((feat, count * cells), jnp.bfloat16),
            pltpu.VMEM((q_local, count * cells, kcount), jnp.bfloat16),
            pltpu.VMEM((q_local, feat * 8, 128), jnp.float32),
            pltpu.VMEM((ROWS * 8, 128), jnp.float32),
            pltpu.VMEM((ROWS * 8, 128), jnp.float32),
            pltpu.VMEM((16, 72, 128), jnp.float32),
            pltpu.VMEM((9, 72, 128), jnp.float32),
            pltpu.VMEM((4, NB, 8, 128), jnp.float32),
            pltpu.VMEM((NB * 8, 128), jnp.float32),
            pltpu.VMEM((NM * 8, 128), jnp.float32),
            pltpu.VMEM((q_local, NB * 8, 128), jnp.bfloat16),
            pltpu.VMEM((8, 128), jnp.float32),
            pltpu.VMEM((cores * q_local, NB * 8, 128), jnp.bfloat16),
            pltpu.VMEM((count, 8, 128), jnp.float32),
            peers,
            peers,
            peers,
            peers,
            peers,
            peers,
            peers,
            peers,
            slots,
            slots,
            peers,
            peers,
            pltpu.SemaphoreType.DMA((1,)),
        ],
        compiler_params=pltpu.CompilerParams(
            collective_id=0, has_side_effects=True, vmem_limit_bytes=60 * 1024 * 1024
        ),
    )(
        modes,
        steps,
        unitary_band_mixer,
        aux,
        localized_matrix_element_table,
        cell_rows,
        freq_own,
    )
    return (self_energy, linewidth)


def solution(mesh):
    return jax.shard_map(
        on_device,
        mesh=mesh,
        in_specs=(
            P(None, "ka"),
            P(),
            P(("grp", "pb"), "ka", None),
            P(None, ("grp", "ka")),
            P(None, ("grp", "ka")),
            P(("grp", "pb"), "ka"),
            P(("grp", "pb"), None),
            P(("grp", "ka")),
            P("grp"),
        ),
        out_specs=(P(None, ("grp", "ka")), P(("grp", "pb"), None)),
        check_vma=False,
    )
```
